256 devices in a mesh: dp: 16 (over y, x_lo, core), head: 16 (over x_hi, z).
Axes of the slice: x: 4 (x_hi: 2, x_lo: 2; x = x_hi * 2 + x_lo), y: 4, z: 8, core: 2. Of those that a mesh axis runs over, the one named last changes fastest.
Arguments:
- query_rows: bfloat16 [16384, 8192], P('dp', 'head'), may hold values from -126 to 126
- key_rows: bfloat16 [16384, 1024], P('dp'), may hold values from -6 to 6
- value_rows: bfloat16 [16384, 1024], P('dp'), may hold values from -6 to 6
- out_weight: bfloat16 [8192, 8192], P('head'), may hold values from -0.0625 to 0.0625
- prompt_lengths: int32 [16, 4], P('dp'), may hold values from 1 to 512, 1024 in all within a row
- cache_pool: bfloat16 [2048, 2, 16, 1024], P('dp', None, None, 'head'), may hold values from -6 to 6
- victim_blocks: int32 [1024], P('dp'), may hold values from 0 to 127
- destinations: int32 [1024, 1], P('dp'), may hold values from 0 to 15; in each aligned block of 64 rows (0 to 63, 64 to 127, ...) at most 8 rows name the same one
- free_slots: int32 [16, 128], P('dp'), may hold values from 0 to 127, each once within a row
Outputs:
- attended: bfloat16 [16384, 8192], P(('dp', 'head'))
- new_pool: bfloat16 [2048, 2, 16, 1024], P('dp', None, None, 'head')
The draws below stay inside these ranges and needn't reach their ends.
Inputs may be any that keep to these rules, and one draw needn't show every extreme that they name: `destinations`: in the 64 victim blocks of one replica no destination is named more than 8 times. `victim_blocks`: pool blocks of the sending replica. `free_slots`: each row is an order of the 128 slots. `prompt_lengths`: each row sums to 1024.
All inputs are finite; a program needn't handle non-finite values.
Results may differ from the reference program's by a relative error of at most 0.019.
Values may be sent and summed in bfloat16 or wider, within the bound.
No kernel may reach another device: no remote copies, remote signals or barrier semaphores. Data moves between devices by JAX's collectives and lax.ppermute only.
A program may use at most 128 MiB of HBM per device.

```python
import math
import jax
import jax.numpy as jnp
import numpy as np
from jax import lax

HD = 128
QH_DEV = 4
HQ = 64
KVH = 8
D_OUT = 8192
TOK = 1024
TOKENS = 16384
NSEG = 4
BT = 16
POOL = 128
VB = 64
CAP = 8
TOTAL_VB = 1024
N_DP = 16
N_HEAD = 16


def base_keys(key):
    return jnp.clip(jax.random.normal(key, (TOKENS, KVH * HD), jnp.float32), -6.0, 6.0)


def draw_key_rows(key, part):
    result = base_keys(key)
    return result.astype(jnp.bfloat16)


def draw_query_rows(key, part):
    own_key = jax.random.fold_in(key, 5)
    result = jnp.clip(jax.random.normal(own_key, (TOKENS, HQ * HD), jnp.float32), -6.0, 6.0)
    return result.astype(jnp.bfloat16)


def touch_ends(entries, rng, least, largest):
    dims = entries.shape
    place = [jax.random.randint(jax.random.fold_in(rng, axis), (), 0, dims[axis]) for axis in range(len(dims))]
    entries = entries.at[tuple(place)].set(least)
    longest = dims.index(max(dims))
    place[longest] = (place[longest] + 1) % dims[longest]
    return entries.at[tuple(place)].set(largest)


def block_scale(stream_key, shape, split, low, largest):
    factor_of, own = 1.0, jax.random.fold_in(stream_key, 6)
    for axis_at, blocks in split:
        draws = jnp.exp(jax.random.uniform(jax.random.fold_in(own, axis_at), (blocks,), jnp.float32, low / len(split), largest / len(split)))
        factor_of = factor_of * jnp.repeat(draws, shape[axis_at] // blocks).reshape([-1 if axis == axis_at else 1 for axis in range(len(shape))])
    return factor_of


def length_profile(number_of, total, limit, skew):
    weights = [(1 << 20) // math.isqrt(standing ** skew) + 1 for standing in range(2, number_of + 1)]
    surplus, given = total - limit - (number_of - 1), [1] * (number_of - 1)
    while surplus > 0:
        movable = [i for i in range(number_of - 1) if given[i] < limit]
        whole, remaining = sum([weights[i] for i in movable]), surplus
        for i in movable:
            more = min(limit - given[i], max(1, remaining * weights[i] // whole), surplus)
            given[i] = given[i] + more
            surplus = surplus - more
    return np.array([limit] + given)


def uneven_parts(key, amount, total, reach, lean):
    if amount == 2:
        one = jax.random.randint(key, (), max(1, total - reach), min(reach, total - 1) + 1)
        return jnp.stack([one, total - one])
    tallies = jnp.asarray(length_profile(amount, total, reach, lean), jnp.int32)
    twos = (amount - 1) // 2
    source_of, taker = tallies[1:1 + 2 * twos:2], tallies[2:2 + 2 * twos:2]
    slack = jnp.minimum(source_of - 1, reach - taker)
    moved = jax.random.randint(jax.random.fold_in(key, 1), (twos,), 0, 1 << 20) % (slack + 1)
    tallies = tallies.at[1:1 + 2 * twos:2].set(source_of - moved).at[2:2 + 2 * twos:2].set(taker + moved)
    return tallies[jax.random.permutation(jax.random.fold_in(key, 2), amount)]


def deal_out(rng, own, number, rows, amount, top, reach, skew):
    sequence = jax.random.permutation(rng, amount)
    packed, common = shares(amount, rows * top, reach, skew, True), shares(amount, rows * top, reach, skew, False)
    places = jnp.arange(amount)

    def named(tallies, rotation):
        used = int((tallies > 0).sum())
        fixed = max(1, used // 4)
        moved = fixed + (places - fixed + rotation * (used - fixed)) % max(1, amount - fixed)
        return jnp.zeros((amount,), jnp.int32).at[sequence[jnp.where(places < fixed, places, moved)]].set(jnp.asarray(tallies, jnp.int32))

    tallies = jnp.where(number % 4 == 0, named(packed, number // 4), named(common, number - number // 4 - 1))
    mixed = jax.random.permutation(jax.random.fold_in(own, 3), amount)
    donor, sink = mixed[0:amount // 2 * 2:2], mixed[1:amount // 2 * 2:2]
    slack = jnp.minimum(tallies[donor] - 1, reach - tallies[sink]) // 2
    slack = jnp.where((donor == sequence[0]) | (sink == sequence[0]) | (tallies[sink] == 0), 0, jnp.maximum(slack, 0))
    moved = jax.random.randint(jax.random.fold_in(own, 4), (amount // 2,), 0, 1 << 20) % (slack + 1)
    tallies = tallies.at[donor].add(-moved).at[sink].add(moved)
    items = jnp.searchsorted(jnp.cumsum(tallies), jnp.arange(rows * top), side="right").astype(jnp.int32)
    grid = items.reshape(top, rows).T
    grid = grid[jax.random.permutation(jax.random.fold_in(own, 1), rows)]
    rotation = jax.random.randint(jax.random.fold_in(own, 2), (rows, 1), 0, top)
    return jnp.take_along_axis(grid, (jnp.arange(top)[None, :] + rotation) % top, axis=1)


def shares(count, total, limit, slope, full):
    weights = [(1 << 20) // math.isqrt(standing ** slope) + 1 for standing in range(1, count + 1)]
    largest = limit if full else min(limit, max(-(-total // count), total * weights[0] // sum(weights)))
    least = 1 if total - largest >= count - 1 else 0
    given, surplus = [largest] + [least] * (count - 1), total - largest - least * (count - 1)
    while surplus > 0:
        movable = [i for i in range(1, count) if given[i] < largest] or [i for i in range(1, count) if given[i] < limit]
        whole, budget = sum([weights[i] for i in movable]), surplus
        for i in movable:
            extra = min(limit - given[i], max(1, budget * weights[i] // whole), surplus)
            given[i] = given[i] + extra
            surplus = surplus - extra
    return np.array(given)


def scatter_about(rng, dims, deviation, bound, pieces=(), kind=jnp.bfloat16):
    loudness = block_scale(rng, dims, pieces, -0.22, 0.18) if pieces else 1.0
    values = jax.random.normal(rng, dims, jnp.float32) * deviation * loudness
    return jnp.minimum(jnp.maximum(values, -bound), bound).astype(kind)


def setup_inputs(seed: int = 0) -> dict:
    arg_keys = jax.random.split(jax.random.key(seed), 10)
    query_rows = draw_query_rows(jax.random.fold_in(arg_keys[9], 71), 0)
    key_rows = draw_key_rows(jax.random.fold_in(arg_keys[9], 71), 0)
    value_rows = scatter_about(arg_keys[2], (TOKENS, KVH * HD), 1.0, 6.0, ((0, 16),))
    out_weight = scatter_about(arg_keys[3], (HQ * HD, D_OUT), (HQ * HD) ** -0.5, 0.0625, ((0, 16),))
    prompt_lengths = jax.vmap(lambda own: uneven_parts(own, NSEG, TOK, TOK // 2, 2))(jax.random.split(arg_keys[4], N_DP)).reshape((N_DP, NSEG)).astype(jnp.int32)
    cache_pool = scatter_about(arg_keys[5], (N_DP * POOL, 2, BT, KVH * HD), 1.0, 6.0, ((0, 16), (3, 16)))
    victim_blocks = touch_ends(jax.random.randint(arg_keys[6], (TOTAL_VB,), 0, POOL), jax.random.fold_in(arg_keys[6], 1), 0, POOL - 1).astype(jnp.int32)
    destinations_keys = jax.random.split(jax.random.fold_in(arg_keys[7], 1), TOTAL_VB // VB)
    destinations_turns = jax.random.permutation(jax.random.fold_in(arg_keys[7], 3), TOTAL_VB // VB)
    destinations = jax.vmap(lambda own, number: deal_out(jax.random.fold_in(arg_keys[7], 2), own, number, VB, N_DP, 1, CAP, 2))(destinations_keys, destinations_turns).reshape((TOTAL_VB, 1))
    free_slots = jax.vmap(lambda own: jax.random.permutation(own, POOL))(jax.random.split(arg_keys[8], N_DP)).reshape((N_DP, POOL)).astype(jnp.int32)
    return dict(query_rows=query_rows, key_rows=key_rows, value_rows=value_rows, out_weight=out_weight, prompt_lengths=prompt_lengths, cache_pool=cache_pool, victim_blocks=victim_blocks, destinations=destinations, free_slots=free_slots)


def segment_ids(lengths_row, count):
    ends = jnp.cumsum(lengths_row)
    places = jnp.arange(count, dtype=jnp.int32)
    return lax.optimization_barrier(jnp.sum((places[:, None] >= ends[None, :]).astype(jnp.int32), axis=1))

def attend_rows(query_rows, key_rows, value_rows, lengths_row):
    count = query_rows.shape[0]
    groups = key_rows.shape[1] // HD
    per = query_rows.shape[1] // HD // groups
    qf = query_rows.astype(jnp.float32).reshape(count, groups, per, HD)
    kf = key_rows.astype(jnp.float32).reshape(count, groups, HD)
    vf = value_rows.astype(jnp.float32).reshape(count, groups, HD)
    scores = jnp.einsum('tgpd,ugd->gptu', qf, kf) / math.sqrt(HD)
    segs = segment_ids(lengths_row, count)
    places = jnp.arange(count, dtype=jnp.int32)
    allowed = (segs[:, None] == segs[None, :]) & (places[:, None] >= places[None, :])
    scores = jnp.where(allowed, scores, jnp.float32(-1e+30))
    top = lax.optimization_barrier(jnp.max(scores, axis=-1, keepdims=True))
    expos = jnp.exp(scores - top)
    total = lax.optimization_barrier(jnp.sum(expos, axis=-1, keepdims=True))
    probs = (expos / total).astype(jnp.bfloat16)
    mixed = jnp.einsum('gptu,ugd->tgpd', probs.astype(jnp.float32), vf)
    return mixed.astype(jnp.bfloat16).reshape(count, groups * per * HD)

def reference(query_rows, key_rows, value_rows, out_weight, prompt_lengths, cache_pool, victim_blocks, destinations, free_slots):

    def one_replica(items):
        return attend_rows(items[0], items[1], items[2], items[3])
    mixed = lax.map(one_replica, (query_rows.reshape(N_DP, TOK, HQ * HD), key_rows.reshape(N_DP, TOK, KVH * HD), value_rows.reshape(N_DP, TOK, KVH * HD), prompt_lengths))
    mixed = mixed.reshape(TOKENS, N_HEAD, QH_DEV * HD).transpose(1, 0, 2)
    weights = out_weight.reshape(N_HEAD, QH_DEV * HD, D_OUT)

    def add_group(total, pair):
        term = jnp.dot(pair[0], pair[1], preferred_element_type=jnp.float32)
        rounded = lax.optimization_barrier(term.astype(jnp.bfloat16))
        return (total + rounded.astype(jnp.float32), None)
    summed, _ = lax.scan(add_group, jnp.zeros((TOKENS, D_OUT), jnp.float32), (mixed, weights))
    attended = summed.astype(jnp.bfloat16)
    written = TOK // BT
    span_keys = key_rows.reshape(N_DP, written, 1, BT, KVH * HD)
    span_values = value_rows.reshape(N_DP, written, 1, BT, KVH * HD)
    span_blocks = jnp.concatenate([span_keys, span_values], axis=2)
    sectioned = cache_pool.reshape(N_DP, POOL, 2, BT, KVH * HD).at[:, :written].set(span_blocks)
    sectioned = sectioned.reshape(N_DP * POOL, 2, BT, KVH * HD)
    targets = destinations[:, 0].astype(jnp.int32)
    onehot = (targets[:, None] == jnp.arange(N_DP, dtype=jnp.int32)[None, :]).astype(jnp.int32)
    before = jnp.cumsum(onehot, axis=0) - onehot
    ranks = lax.optimization_barrier(jnp.sum(before * onehot, axis=1)).astype(jnp.int32)
    slots = free_slots[targets, ranks].astype(jnp.int32)
    sources = jnp.arange(TOTAL_VB, dtype=jnp.int32) // VB * POOL + victim_blocks.astype(jnp.int32)
    places = targets * POOL + slots
    new_pool = sectioned.at[places].set(sectioned[sources])
    return (attended, new_pool)
```

```python
import math

import jax
import jax.numpy as jnp
from jax import lax
from jax.experimental import pallas as pl
from jax.experimental.pallas import tpu as pltpu
from jax.sharding import PartitionSpec as P

HD = 128
KVH = 8
BT = 16
NZ = 8
NY = 4
QB = 256
SPAN = 768
CHUNKS = ((0, 2048), (2048, 2048), (4096, 4096))
BF = jnp.bfloat16
F32 = jnp.float32
X_SWAP = [(i, (i + 8) % 16) for i in range(16)]
CORE_SWAP = [(i, i ^ 1) for i in range(16)]
LO_SWAP = [(i, i ^ 2) for i in range(16)]


def z_shift(k):
    return [(a * NZ + z, a * NZ + (z + k) % NZ) for a in range(2) for z in range(NZ)]


def y_shift(k):
    return [(y * 4 + r, (y + k) % NY * 4 + r) for y in range(NY) for r in range(4)]


def attend_kernel(info, q_ref, k_ref, v_ref, o_ref):
    block = info[0] * 2 + pl.program_id(0)
    base = jnp.maximum(block - 2, 0) * QB
    rows = block * QB + lax.broadcasted_iota(jnp.int32, (QB, 1), 0)
    start = jnp.zeros((QB, 1), jnp.int32)
    for s in range(4):
        start = jnp.where(rows >= info[2 + s], info[2 + s], start)
    cols = base + lax.broadcasted_iota(jnp.int32, (QB, SPAN), 1)
    bias = jnp.where((cols >= start) & (cols <= rows), 0.0, -1e30)
    keys = k_ref[pl.ds(pl.multiple_of(base, QB), SPAN), :]
    values = v_ref[pl.ds(pl.multiple_of(base, QB), SPAN), :]
    for h in range(q_ref.shape[1] // HD):
        q = q_ref[:, h * HD : (h + 1) * HD]
        s = lax.dot_general(q, keys, (((1,), (1,)), ((), ())), preferred_element_type=F32) + bias
        top = jnp.max(s, axis=1, keepdims=True)
        e = jnp.exp((s - top) * (1.0 / math.sqrt(HD)))
        total = jnp.sum(e, axis=1, keepdims=True)
        o = jnp.dot(e.astype(BF), values, preferred_element_type=F32)
        o_ref[:, h * HD : (h + 1) * HD] = (o / total).astype(BF)


def attend_half(info, query_rows, key_rows, value_rows):
    count, width = query_rows.shape
    return pl.pallas_call(
        attend_kernel,
        grid_spec=pltpu.PrefetchScalarGridSpec(
            num_scalar_prefetch=1,
            grid=(2,),
            in_specs=[
                pl.BlockSpec((QB, width), lambda i, info: (info[0] * 2 + i, 0)),
                pl.BlockSpec((count, HD), lambda i, info: (0, info[1])),
                pl.BlockSpec((count, HD), lambda i, info: (0, info[1])),
            ],
            out_specs=pl.BlockSpec((QB, width), lambda i, info: (i, 0)),
        ),
        out_shape=jax.ShapeDtypeStruct((2 * QB, width), BF),
        compiler_params=pltpu.CompilerParams(vmem_limit_bytes=32 * 1024 * 1024),
        cost_estimate=pl.CostEstimate(
            flops=4 * 2 * QB * SPAN * width, bytes_accessed=2 << 20, transcendentals=8 * QB * SPAN
        ),
    )(info, query_rows, key_rows, value_rows)


def partner_columns(out_weight, y, core, first, size):
    depth, part = out_weight.shape[0], size // 8
    mine = lax.dynamic_slice(out_weight, (0, first + (y * 2 + core) * part), (depth, part))
    got = lax.ppermute(mine, "head", X_SWAP)
    near = lax.ppermute(got, "dp", y_shift(1))
    far = lax.ppermute(got, "dp", y_shift(-1))
    across = lax.ppermute(got, "dp", y_shift(2))
    own = jnp.concatenate([got, far, across, near], axis=1)
    other = lax.ppermute(own, "dp", CORE_SWAP)
    full = jnp.zeros((depth, size), BF)
    for j in range(NY):
        for k, source in ((core, own), (1 - core, other)):
            at = ((y + j) % NY * 2 + k) * part
            full = lax.dynamic_update_slice(full, source[:, j * part : (j + 1) * part], (0, at))
    return full


def ring(part, z):
    n = part.shape[2] // 2
    outs = []
    for b, step in ((0, 1), (1, -1)):

        def term(at):
            return lax.dynamic_index_in_dim(part, at % NZ, 0, False)[:, b * n : (b + 1) * n]

        acc = term(z - step)
        for s in range(NZ - 1):
            came = lax.ppermute(acc, "head", z_shift(step))
            acc = (came.astype(F32) + term(z - step * (2 + s)).astype(F32)).astype(BF)
        outs.append(acc)
    return outs


def migrate(key_rows, value_rows, cache_pool, victim_blocks, targets, free_order):
    count, width = key_rows.shape[0], cache_pool.shape[3]
    pool, written = cache_pool.shape[0], count // BT
    at = lax.axis_index("head") * width
    me = lax.axis_index("dp")
    y, low = me // 4, me % 4
    span = jnp.stack(
        [lax.dynamic_slice_in_dim(a, at, width, 1).reshape(written, BT, width) for a in (key_rows, value_rows)],
        axis=1,
    )
    r = jnp.arange(16, dtype=jnp.int32)
    target_place = ((targets // 4 - y) % NY) * 4 + ((targets % 4) ^ low)
    same = targets[:, None] == targets[None, :]
    victims = victim_blocks.shape[0]
    order = jnp.arange(victims, dtype=jnp.int32)
    local_rank = jnp.sum((same & (order[None, :] < order[:, None])).astype(jnp.int32), axis=1)
    slot_of = target_place * 8 + local_rank
    lanes = jnp.arange(128, dtype=jnp.int32)
    picks = (slot_of[None, :] == lanes[:, None]).astype(BF)
    blocks = (victim_blocks[:, None] == jnp.arange(pool, dtype=jnp.int32)[None, :]).astype(BF)
    pick = jnp.dot(picks, blocks, preferred_element_type=F32).astype(BF)
    empty = 1.0 - jnp.sum(pick.astype(F32), axis=1)
    sending = jnp.einsum("sb,bktf->sktf", pick[:, :written], span, preferred_element_type=F32)
    sending = sending + jnp.einsum("sb,bktf->sktf", pick[:, written:], cache_pool[written:], preferred_element_type=F32)
    sending = (sending + 256.0 * empty[:, None, None, None]).astype(BF)
    b = sending.reshape(NY, 2, 2, 8 * 2 * BT * width)
    b = jnp.stack([b[:, :, 0], lax.ppermute(b[:, :, 1], "dp", CORE_SWAP)], axis=2)
    b = jnp.stack([b[:, 0], lax.ppermute(b[:, 1], "dp", LO_SWAP)], axis=1)
    b = jnp.stack([b[0]] + [lax.ppermute(b[k], "dp", y_shift(k)) for k in (1, 2, 3)])
    arrived = b.reshape(128, 2, BT, width)
    valid = (arrived[:, 0, 0, 0].astype(F32) < 100.0).reshape(16, 8)
    source = ((y - r // 4) % NY) * 4 + ((r % 4) ^ low)
    counts = jnp.sum(valid.astype(jnp.int32), axis=1)
    before = jnp.sum(jnp.where(source[None, :] < source[:, None], counts[None, :], 0), axis=1)
    ranks = before[:, None] + jnp.arange(8, dtype=jnp.int32)[None, :]
    rank_of_slot = jnp.sum(
        (free_order[None, :] == jnp.arange(pool, dtype=jnp.int32)[:, None]) * jnp.arange(pool, dtype=jnp.int32)[None, :],
        axis=1,
    )
    hits = (ranks.reshape(128, 1) == rank_of_slot[None, :]) & valid.reshape(128, 1)
    taken = jnp.sum(hits.astype(jnp.int32), axis=0) > 0
    fresh = jnp.einsum(
        "sktf,sb->bktf", jnp.where(valid.reshape(128, 1, 1, 1), arrived, 0), hits.astype(BF), preferred_element_type=F32
    ).astype(BF)
    sectioned = lax.dynamic_update_slice_in_dim(cache_pool, span, 0, 0)
    return jnp.where(taken[:, None, None, None], fresh, sectioned)


def on_device(
    query_rows,
    key_rows,
    value_rows,
    out_weight,
    prompt_lengths,
    cache_pool,
    victim_blocks,
    destinations,
    free_slots,
):
    head, me = lax.axis_index("head"), lax.axis_index("dp")
    z, hi = head % NZ, head // NZ
    y, core = me // 4, me % 2
    local_heads = query_rows.shape[1] // HD
    kv = head * local_heads // (local_heads * lax.axis_size("head") // KVH)
    ends = jnp.cumsum(prompt_lengths[0])
    theirs = jnp.concatenate([jnp.stack([1 - hi, kv]), ends]).astype(jnp.int32)
    ours = jnp.concatenate([jnp.stack([hi, kv]), ends]).astype(jnp.int32)
    given = lax.ppermute(attend_half(theirs, query_rows, key_rows, value_rows), "head", X_SWAP)
    kept = attend_half(ours, query_rows, key_rows, value_rows)
    pieces = []
    for first, size in CHUNKS:
        w = partner_columns(out_weight, y, core, first, size)
        part = jnp.dot(kept, out_weight[:, first : first + size], preferred_element_type=F32)
        part = part + jnp.dot(given, w, preferred_element_type=F32)
        part = part.astype(BF).reshape(NZ, -1, size)
        pieces += ring(part, z)
    attended = jnp.concatenate(pieces, axis=1)
    new_pool = migrate(key_rows, value_rows, cache_pool, victim_blocks, destinations[:, 0], free_slots[0])
    return (attended, new_pool)


def solution(mesh):
    return jax.shard_map(
        on_device,
        mesh=mesh,
        in_specs=(
            P("dp", "head"),
            P("dp", None),
            P("dp", None),
            P("head", None),
            P("dp", None),
            P("dp", None, None, "head"),
            P("dp"),
            P("dp", None),
            P("dp", None),
        ),
        out_specs=(P(("dp", "head"), None), P("dp", None, None, "head")),
        check_vma=False,
    )
```

```python
import functools
import math

import jax
import jax.numpy as jnp
from jax import lax
from jax.experimental import pallas as pl
from jax.experimental.pallas import tpu as pltpu
from jax.sharding import PartitionSpec as P

HD = 128
KVH = 8
BT = 16
NZ = 8
NY = 4
QB = 256
SPAN = 768
FIRST = 2048
GROUPS = ((2048, 5120), (5120, 8192))
Z_GROUPS = [[a * 8 + z for z in range(8)] for a in range(2)]
TILE = 1024
VMEM = 56 * 1024 * 1024
BF = jnp.bfloat16
F32 = jnp.float32
X_SWAP = [(i, (i + 8) % 16) for i in range(16)]
CORE_SWAP = [(i, i ^ 1) for i in range(16)]
LO_SWAP = [(i, i ^ 2) for i in range(16)]

def y_shift(k):
    return [(y * 4 + r, (y + k) % NY * 4 + r) for y in range(NY) for r in range(4)]


def attend_kernel(side, info, lengths, q_ref, k_ref, v_ref, o_ref):
    block = info[side] * 2 + pl.program_id(0)

    def attend(span):
        base = jnp.maximum(block - 2, 0) * QB
        rows = block * QB + lax.broadcasted_iota(jnp.int32, (QB, 1), 0)
        start = jnp.zeros((QB, 1), jnp.int32)
        end = 0
        for s in range(lengths.shape[1]):
            end = end + lengths[0, s]
            start = jnp.where(rows >= end, end, start)
        cols = base + lax.broadcasted_iota(jnp.int32, (QB, span), 1)
        bias = jnp.where((cols >= start) & (cols <= rows), 0.0, -1e30)
        keys = k_ref[pl.ds(pl.multiple_of(base, QB), span), :]
        values = jnp.concatenate(
            [v_ref[pl.ds(pl.multiple_of(base, QB), span), :], jnp.ones((span, HD), BF)], axis=1
        )
        for h in range(q_ref.shape[1] // HD):
            q = q_ref[:, h * HD : (h + 1) * HD]
            s = lax.dot_general(q, keys, (((1,), (1,)), ((), ())), preferred_element_type=F32) + bias
            top = jnp.max(s, axis=1, keepdims=True)
            e = jnp.exp2((s - top) * (math.log2(math.e) / math.sqrt(HD)))
            o = jnp.dot(e.astype(BF), values, preferred_element_type=F32)
            o_ref[:, h * HD : (h + 1) * HD] = (o[:, :HD] / o[:, HD:]).astype(BF)

    pl.when(block == 0)(lambda: attend(QB))
    pl.when(block == 1)(lambda: attend(2 * QB))
    pl.when(block >= 2)(lambda: attend(SPAN))


def attend_half(side, info, prompt_lengths, query_rows, key_rows, value_rows):
    count, width = query_rows.shape
    return pl.pallas_call(
        functools.partial(attend_kernel, side),
        grid_spec=pltpu.PrefetchScalarGridSpec(
            num_scalar_prefetch=2,
            grid=(2,),
            in_specs=[
                pl.BlockSpec((QB, width), lambda i, info, _: (info[side] * 2 + i, 0)),
                pl.BlockSpec((count, HD), lambda i, info, _: (0, info[2])),
                pl.BlockSpec((count, HD), lambda i, info, _: (0, info[2])),
            ],
            out_specs=pl.BlockSpec((QB, width), lambda i, info, _: (i, 0)),
        ),
        out_shape=jax.ShapeDtypeStruct((2 * QB, width), BF),
        compiler_params=pltpu.CompilerParams(vmem_limit_bytes=VMEM),
        cost_estimate=pl.CostEstimate(
            flops=4 * 2 * QB * SPAN * width, bytes_accessed=2 << 20, transcendentals=8 * QB * SPAN
        ),
    )(info, prompt_lengths, query_rows, key_rows, value_rows)


def after(value, *earlier):
    return lax.optimization_barrier((value, *earlier))[0]


def project_kernel(kept_ref, given_ref, w_ref, own_ref, other_ref, *refs):
    o_ref = refs[-1]
    half = own_ref.shape[0]
    acc = jnp.dot(kept_ref[...], w_ref[...], preferred_element_type=F32)
    acc += jnp.dot(given_ref[:, :half], own_ref[...], preferred_element_type=F32)
    acc += jnp.dot(given_ref[:, half:], other_ref[...], preferred_element_type=F32)
    o_ref[...] = acc.astype(BF)


def project(kept, given, out_weight, group, own, other, filled):
    rows, depth = kept.shape
    first, last = GROUPS[group]
    base = GROUPS[0][0]
    return pl.pallas_call(
        project_kernel,
        grid=((last - first) // TILE,),
        in_specs=[
            pl.BlockSpec((rows, depth), lambda i: (0, 0)),
            pl.BlockSpec((rows, depth), lambda i: (0, 0)),
            pl.BlockSpec((depth, TILE), lambda i: (0, first // TILE + i)),
            pl.BlockSpec((depth // 2, TILE), lambda i: (0, i)),
            pl.BlockSpec((depth // 2, TILE), lambda i: (0, i)),
        ]
        + [pl.BlockSpec(memory_space=pl.ANY)] * len(filled),
        out_specs=pl.BlockSpec((rows, TILE), lambda i: (0, (first - base) // TILE + i)),
        out_shape=jax.ShapeDtypeStruct((rows, GROUPS[-1][1] - base), BF),
        input_output_aliases={5: 0} if filled else {},
        compiler_params=pltpu.CompilerParams(vmem_limit_bytes=VMEM),
        cost_estimate=pl.CostEstimate(
            flops=4 * rows * depth * (last - first), bytes_accessed=6 * depth * (last - first), transcendentals=0
        ),
    )(kept, given, out_weight, own, other, *filled)


def project_first_kernel(kept_ref, theirs_ref, w_ref, o_ref):
    own = pl.program_id(0) == 0
    rows = jnp.where(own, kept_ref[...], theirs_ref[...])
    o_ref[...] = jnp.dot(rows, w_ref[...], preferred_element_type=F32).astype(BF)


def project_first(kept, theirs, out_weight, size):
    rows, depth = kept.shape
    tiles = size // TILE
    return pl.pallas_call(
        project_first_kernel,
        grid=(2, tiles),
        in_specs=[
            pl.BlockSpec((rows, depth), lambda h, i: (0, 0)),
            pl.BlockSpec((rows, depth), lambda h, i: (0, 0)),
            pl.BlockSpec((depth, TILE), lambda h, i: (0, i)),
        ],
        out_specs=pl.BlockSpec((rows, TILE), lambda h, i: (0, h * tiles + i)),
        out_shape=jax.ShapeDtypeStruct((rows, 2 * size), BF),
        compiler_params=pltpu.CompilerParams(vmem_limit_bytes=VMEM),
        cost_estimate=pl.CostEstimate(
            flops=4 * rows * depth * size, bytes_accessed=3 * depth * size * 2, transcendentals=0
        ),
    )(kept, theirs, out_weight)


def sum_over_z(part):
    return lax.psum_scatter(part, "head", scatter_dimension=0, axis_index_groups=Z_GROUPS, tiled=True)


def migrate(key_rows, value_rows, cache_pool, victim_blocks, targets, free_order):
    count, width = key_rows.shape[0], cache_pool.shape[3]
    pool, written = cache_pool.shape[0], count // BT
    at = lax.axis_index("head") * width
    me = lax.axis_index("dp")
    y, low = me // 4, me % 4
    rows = [after(lax.dynamic_slice_in_dim(a, at, width, 1), targets) for a in (key_rows, value_rows)]
    span = jnp.stack([a.reshape(written, BT, width) for a in rows], axis=1)
    r = jnp.arange(16, dtype=jnp.int32)
    target_place = ((targets // 4 - y) % NY) * 4 + ((targets % 4) ^ low)
    same = targets[:, None] == targets[None, :]
    victims = victim_blocks.shape[0]
    order = jnp.arange(victims, dtype=jnp.int32)
    local_rank = jnp.sum((same & (order[None, :] < order[:, None])).astype(jnp.int32), axis=1)
    slot_of = target_place * 8 + local_rank
    lanes = jnp.arange(128, dtype=jnp.int32)
    picks = (slot_of[None, :] == lanes[:, None]).astype(BF)
    blocks = (victim_blocks[:, None] == jnp.arange(pool, dtype=jnp.int32)[None, :]).astype(BF)
    pick = jnp.dot(picks, blocks, preferred_element_type=F32).astype(BF)
    empty = 1.0 - jnp.sum(pick.astype(F32), axis=1)
    sending = jnp.einsum("sb,bktf->sktf", pick[:, :written], span, preferred_element_type=F32)
    sending = sending + jnp.einsum("sb,bktf->sktf", pick[:, written:], cache_pool[written:], preferred_element_type=F32)
    sending = (sending + 256.0 * empty[:, None, None, None]).astype(BF)
    b = sending.reshape(NY, 2, 2, 8 * 2 * BT * width)
    b = jnp.stack([b[:, :, 0], lax.ppermute(b[:, :, 1], "dp", CORE_SWAP)], axis=2)
    b = jnp.stack([b[:, 0], lax.ppermute(b[:, 1], "dp", LO_SWAP)], axis=1)
    b = jnp.stack([b[0]] + [lax.ppermute(b[k], "dp", y_shift(k)) for k in (1, 2, 3)])
    arrived = b.reshape(128, 2, BT, width)
    valid = (arrived[:, 0, 0, 0].astype(F32) < 100.0).reshape(16, 8)
    source = ((y - r // 4) % NY) * 4 + ((r % 4) ^ low)
    counts = jnp.sum(valid.astype(jnp.int32), axis=1)
    before = jnp.sum(jnp.where(source[None, :] < source[:, None], counts[None, :], 0), axis=1)
    ranks = before[:, None] + jnp.arange(8, dtype=jnp.int32)[None, :]
    rank_of_slot = jnp.sum(
        (free_order[None, :] == jnp.arange(pool, dtype=jnp.int32)[:, None]) * jnp.arange(pool, dtype=jnp.int32)[None, :],
        axis=1,
    )
    hits = (ranks.reshape(128, 1) == rank_of_slot[None, :]) & valid.reshape(128, 1)
    taken = jnp.sum(hits.astype(jnp.int32), axis=0) > 0
    fresh = jnp.einsum(
        "sktf,sb->bktf", jnp.where(valid.reshape(128, 1, 1, 1), arrived, 0), hits.astype(BF), preferred_element_type=F32
    ).astype(BF)
    sectioned = lax.dynamic_update_slice_in_dim(cache_pool, span, 0, 0)
    return jnp.where(taken[:, None, None, None], fresh, sectioned)


def on_device(
    query_rows,
    key_rows,
    value_rows,
    out_weight,
    prompt_lengths,
    cache_pool,
    victim_blocks,
    destinations,
    free_slots,
):
    head, me = lax.axis_index("head"), lax.axis_index("dp")
    z, hi = head % NZ, head // NZ
    y, core = me // 4, me % 2
    depth = out_weight.shape[0]
    eighth = depth // 8
    slab = lax.dynamic_slice_in_dim(out_weight, (y * 2 + core) * eighth, eighth, 0)
    kv = head * KVH // lax.axis_size("head")
    place = jnp.arange(depth, dtype=jnp.int32)
    slot = place // eighth
    taken_from = (((y + slot % NY) % NY) * 2 + (core ^ (slot // NY))) * eighth + place % eighth
    order = (place[:, None] == taken_from[None, :]).astype(BF)
    info = jnp.stack([1 - hi, hi, kv])
    count = query_rows.shape[0] // 2
    got = [lax.ppermute(slab[:, slice(*GROUPS[0])], "head", X_SWAP)]
    opposite = lax.dynamic_slice_in_dim(after(out_weight, got[0]), ((y + 2) % NY * 2 + core) * eighth, eighth, 0)
    theirs = attend_half(0, info, prompt_lengths, query_rows, key_rows, value_rows)
    came = lax.ppermute(theirs, "head", X_SWAP)
    kept = attend_half(1, info, after(prompt_lengths, theirs, got[0]), query_rows, key_rows, value_rows)
    given = jnp.dot(came, order, preferred_element_type=F32).astype(BF)
    part = project_first(kept, theirs, out_weight, FIRST)
    firsts = sum_over_z(part).reshape(count // NZ, 2 * FIRST)
    both = jnp.concatenate([slab[:, slice(*GROUPS[1])], opposite[:, slice(*GROUPS[1])]], axis=0)
    got.append(lax.ppermute(after(both, got[0]), "head", X_SWAP))
    sides, before = [], ()
    for i in range(len(GROUPS)):
        piece, across = got[i][:eighth], got[i][eighth:]
        piece = after(piece, theirs, *before)
        near, far = (lax.ppermute(piece, "dp", y_shift(k)) for k in (1, -1))
        if i == 0:
            across = lax.ppermute(piece, "dp", y_shift(2))
        before = (near, far, across)
        own = after(jnp.concatenate([piece, far, across, near], axis=0), came)
        sides.append((own, lax.ppermute(own, "dp", CORE_SWAP)))
    part = project(kept, after(given, got[1], *before), out_weight, 0, *sides[0], ())
    part = project(kept, given, out_weight, 1, *sides[1], (part,))
    rest = sum_over_z(part)
    swapped = lax.ppermute(firsts[:, FIRST:], "head", X_SWAP)
    begin = (firsts[:, :FIRST].astype(F32) + swapped.astype(F32)).astype(BF)
    attended = jnp.zeros((count // NZ, out_weight.shape[1]), BF)
    for lo, piece in ((0, begin), (FIRST, rest)):
        attended = lax.dynamic_update_slice(attended, piece, (0, lo))
    victim_blocks, targets, free_order, _ = lax.optimization_barrier(
        (victim_blocks, destinations[:, 0], free_slots[0], part)
    )
    new_pool = migrate(key_rows, value_rows, cache_pool, victim_blocks, targets, free_order)
    return (attended, new_pool)


def solution(mesh):
    return jax.shard_map(
        on_device,
        mesh=mesh,
        in_specs=(
            P("dp", "head"),
            P("dp", None),
            P("dp", None),
            P("head", None),
            P("dp", None),
            P("dp", None, None, "head"),
            P("dp"),
            P("dp", None),
            P("dp", None),
        ),
        out_specs=(P(("dp", "head"), None), P("dp", None, None, "head")),
        check_vma=False,
    )
```

```python
import functools
import math

import jax
import jax.numpy as jnp
from jax import lax
from jax.experimental import pallas as pl
from jax.experimental.pallas import tpu as pltpu
from jax.sharding import PartitionSpec as P

HD = 128
KVH = 8
BT = 16
NZ = 8
NY = 4
QB = 256
SPAN = 768
FIRST = 2048
GROUPS = ((2048, 5120), (5120, 8192))
Z_GROUPS = [[a * 8 + z for z in range(8)] for a in range(2)]
TILE = 1024
VMEM = 56 * 1024 * 1024
BF = jnp.bfloat16
F32 = jnp.float32
X_SWAP = [(i, (i + 8) % 16) for i in range(16)]
CORE_SWAP = [(i, i ^ 1) for i in range(16)]
LO_SWAP = [(i, i ^ 2) for i in range(16)]

def y_shift(k):
    return [(y * 4 + r, (y + k) % NY * 4 + r) for y in range(NY) for r in range(4)]


def attend_kernel(side, info, lengths, q_ref, k_ref, v_ref, o_ref):
    block = info[side] * 2 + pl.program_id(0)

    def attend(span):
        base = jnp.maximum(block - 2, 0) * QB
        rows = block * QB + lax.broadcasted_iota(jnp.int32, (QB, 1), 0)
        start = jnp.zeros((QB, 1), jnp.int32)
        end = 0
        for s in range(lengths.shape[1]):
            end = end + lengths[0, s]
            start = jnp.where(rows >= end, end, start)
        cols = base + lax.broadcasted_iota(jnp.int32, (QB, span), 1)
        bias = jnp.where((cols >= start) & (cols <= rows), 0.0, -1e30)
        keys = k_ref[pl.ds(pl.multiple_of(base, QB), span), :]
        values = jnp.concatenate(
            [v_ref[pl.ds(pl.multiple_of(base, QB), span), :], jnp.ones((span, HD), BF)], axis=1
        )
        for h in range(q_ref.shape[1] // HD):
            q = q_ref[:, h * HD : (h + 1) * HD]
            s = lax.dot_general(q, keys, (((1,), (1,)), ((), ())), preferred_element_type=F32) + bias
            top = jnp.max(s, axis=1, keepdims=True)
            e = jnp.exp2((s - top) * (math.log2(math.e) / math.sqrt(HD)))
            o = jnp.dot(e.astype(BF), values, preferred_element_type=F32)
            o_ref[:, h * HD : (h + 1) * HD] = (o[:, :HD] / o[:, HD:]).astype(BF)

    pl.when(block == 0)(lambda: attend(QB))
    pl.when(block == 1)(lambda: attend(2 * QB))
    pl.when(block >= 2)(lambda: attend(SPAN))


def attend_half(side, info, prompt_lengths, query_rows, key_rows, value_rows):
    count, width = query_rows.shape
    return pl.pallas_call(
        functools.partial(attend_kernel, side),
        grid_spec=pltpu.PrefetchScalarGridSpec(
            num_scalar_prefetch=2,
            grid=(2,),
            in_specs=[
                pl.BlockSpec((QB, width), lambda i, info, _: (info[side] * 2 + i, 0)),
                pl.BlockSpec((count, HD), lambda i, info, _: (0, info[2])),
                pl.BlockSpec((count, HD), lambda i, info, _: (0, info[2])),
            ],
            out_specs=pl.BlockSpec((QB, width), lambda i, info, _: (i, 0)),
        ),
        out_shape=jax.ShapeDtypeStruct((2 * QB, width), BF),
        compiler_params=pltpu.CompilerParams(vmem_limit_bytes=VMEM),
        cost_estimate=pl.CostEstimate(
            flops=4 * 2 * QB * SPAN * width, bytes_accessed=2 << 20, transcendentals=8 * QB * SPAN
        ),
    )(info, prompt_lengths, query_rows, key_rows, value_rows)


def after(value, *earlier):
    return lax.optimization_barrier((value, *earlier))[0]


def project_kernel(kept_ref, given_ref, w_ref, own_ref, other_ref, *refs):
    o_ref = refs[-1]
    half = own_ref.shape[0]
    acc = jnp.dot(kept_ref[...], w_ref[...], preferred_element_type=F32)
    acc += jnp.dot(given_ref[:, :half], own_ref[...], preferred_element_type=F32)
    acc += jnp.dot(given_ref[:, half:], other_ref[...], preferred_element_type=F32)
    o_ref[...] = acc.astype(BF)


def project(kept, given, out_weight, group, own, other, filled):
    rows, depth = kept.shape
    first, last = GROUPS[group]
    base = GROUPS[0][0]
    return pl.pallas_call(
        project_kernel,
        grid=((last - first) // TILE,),
        in_specs=[
            pl.BlockSpec((rows, depth), lambda i: (0, 0)),
            pl.BlockSpec((rows, depth), lambda i: (0, 0)),
            pl.BlockSpec((depth, TILE), lambda i: (0, first // TILE + i)),
            pl.BlockSpec((depth // 2, TILE), lambda i: (0, i)),
            pl.BlockSpec((depth // 2, TILE), lambda i: (0, i)),
        ]
        + [pl.BlockSpec(memory_space=pl.ANY)] * len(filled),
        out_specs=pl.BlockSpec((rows, TILE), lambda i: (0, (first - base) // TILE + i)),
        out_shape=jax.ShapeDtypeStruct((rows, GROUPS[-1][1] - base), BF),
        input_output_aliases={5: 0} if filled else {},
        compiler_params=pltpu.CompilerParams(vmem_limit_bytes=VMEM),
        cost_estimate=pl.CostEstimate(
            flops=4 * rows * depth * (last - first), bytes_accessed=6 * depth * (last - first), transcendentals=0
        ),
    )(kept, given, out_weight, own, other, *filled)


def project_first_kernel(kept_ref, theirs_ref, w_ref, o_ref):
    own = pl.program_id(0) == 0
    rows = jnp.where(own, kept_ref[...], theirs_ref[...])
    o_ref[...] = jnp.dot(rows, w_ref[...], preferred_element_type=F32).astype(BF)


def project_first(kept, theirs, out_weight, size):
    rows, depth = kept.shape
    tiles = size // TILE
    return pl.pallas_call(
        project_first_kernel,
        grid=(2, tiles),
        in_specs=[
            pl.BlockSpec((rows, depth), lambda h, i: (0, 0)),
            pl.BlockSpec((rows, depth), lambda h, i: (0, 0)),
            pl.BlockSpec((depth, TILE), lambda h, i: (0, i)),
        ],
        out_specs=pl.BlockSpec((rows, TILE), lambda h, i: (0, h * tiles + i)),
        out_shape=jax.ShapeDtypeStruct((rows, 2 * size), BF),
        compiler_params=pltpu.CompilerParams(vmem_limit_bytes=VMEM),
        cost_estimate=pl.CostEstimate(
            flops=4 * rows * depth * size, bytes_accessed=3 * depth * size * 2, transcendentals=0
        ),
    )(kept, theirs, out_weight)


def sum_over_z(part):
    return lax.psum_scatter(part, "head", scatter_dimension=0, axis_index_groups=Z_GROUPS, tiled=True)


def migrate(key_rows, value_rows, cache_pool, victim_blocks, targets, free_order):
    count, width = key_rows.shape[0], cache_pool.shape[3]
    pool, written = cache_pool.shape[0], count // BT
    at = lax.axis_index("head") * width
    me = lax.axis_index("dp")
    y, low = me // 4, me % 4
    at, half = after(jnp.stack([at, jnp.int32(written)]), targets)
    rows = [lax.dynamic_slice_in_dim(a, at, width, 1) for a in (key_rows, value_rows)]
    unwritten = lax.dynamic_slice_in_dim(cache_pool, half, pool - written, 0)
    span = jnp.stack([a.reshape(written, BT, width) for a in rows], axis=1)
    r = jnp.arange(16, dtype=jnp.int32)
    target_place = ((targets // 4 - y) % NY) * 4 + ((targets % 4) ^ low)
    same = targets[:, None] == targets[None, :]
    victims = victim_blocks.shape[0]
    order = jnp.arange(victims, dtype=jnp.int32)
    local_rank = jnp.sum((same & (order[None, :] < order[:, None])).astype(jnp.int32), axis=1)
    slot_of = target_place * 8 + local_rank
    lanes = jnp.arange(128, dtype=jnp.int32)
    picks = (slot_of[None, :] == lanes[:, None]).astype(BF)
    blocks = (victim_blocks[:, None] == jnp.arange(pool, dtype=jnp.int32)[None, :]).astype(BF)
    pick = jnp.dot(picks, blocks, preferred_element_type=F32).astype(BF)
    empty = 1.0 - jnp.sum(pick.astype(F32), axis=1)
    sending = jnp.einsum("sb,bktf->sktf", pick[:, :written], span, preferred_element_type=F32)
    sending = sending + jnp.einsum("sb,bktf->sktf", pick[:, written:], unwritten, preferred_element_type=F32)
    sending = (sending + 256.0 * empty[:, None, None, None]).astype(BF)
    b = sending.reshape(NY, 2, 2, 8 * 2 * BT * width)
    b = jnp.stack([b[:, :, 0], lax.ppermute(b[:, :, 1], "dp", CORE_SWAP)], axis=2)
    b = jnp.stack([b[:, 0], lax.ppermute(b[:, 1], "dp", LO_SWAP)], axis=1)
    b = jnp.stack([b[0]] + [lax.ppermute(b[k], "dp", y_shift(k)) for k in (1, 2, 3)])
    arrived = b.reshape(128, 2, BT, width)
    valid = (arrived[:, 0, 0, 0].astype(F32) < 100.0).reshape(16, 8)
    source = ((y - r // 4) % NY) * 4 + ((r % 4) ^ low)
    counts = jnp.sum(valid.astype(jnp.int32), axis=1)
    before = jnp.sum(jnp.where(source[None, :] < source[:, None], counts[None, :], 0), axis=1)
    ranks = before[:, None] + jnp.arange(8, dtype=jnp.int32)[None, :]
    rank_of_slot = jnp.sum(
        (free_order[None, :] == jnp.arange(pool, dtype=jnp.int32)[:, None]) * jnp.arange(pool, dtype=jnp.int32)[None, :],
        axis=1,
    )
    hits = (ranks.reshape(128, 1) == rank_of_slot[None, :]) & valid.reshape(128, 1)
    taken = jnp.sum(hits.astype(jnp.int32), axis=0) > 0
    fresh = jnp.einsum(
        "sktf,sb->bktf", jnp.where(valid.reshape(128, 1, 1, 1), arrived, 0), hits.astype(BF), preferred_element_type=F32
    ).astype(BF)
    sectioned = jnp.concatenate([span, unwritten], axis=0)
    return jnp.where(taken[:, None, None, None], fresh, sectioned)


def on_device(
    query_rows,
    key_rows,
    value_rows,
    out_weight,
    prompt_lengths,
    cache_pool,
    victim_blocks,
    destinations,
    free_slots,
):
    head, me = lax.axis_index("head"), lax.axis_index("dp")
    z, hi = head % NZ, head // NZ
    y, core = me // 4, me % 2
    depth = out_weight.shape[0]
    eighth = depth // 8
    slab = lax.dynamic_slice_in_dim(out_weight, (y * 2 + core) * eighth, eighth, 0)
    kv = head * KVH // lax.axis_size("head")
    place = jnp.arange(depth, dtype=jnp.int32)
    slot = place // eighth
    taken_from = (((y + slot % NY) % NY) * 2 + (core ^ (slot // NY))) * eighth + place % eighth
    order = (place[:, None] == taken_from[None, :]).astype(BF)
    info = jnp.stack([1 - hi, hi, kv])
    count = query_rows.shape[0] // 2
    got = [lax.ppermute(slab[:, slice(*GROUPS[0])], "head", X_SWAP)]
    opposite = lax.dynamic_slice_in_dim(after(out_weight, got[0]), ((y + 2) % NY * 2 + core) * eighth, eighth, 0)
    theirs = attend_half(0, info, prompt_lengths, query_rows, key_rows, value_rows)
    came = lax.ppermute(theirs, "head", X_SWAP)
    kept = attend_half(1, info, after(prompt_lengths, theirs), query_rows, key_rows, value_rows)
    given = jnp.dot(came, order, preferred_element_type=F32).astype(BF)
    part = project_first(kept, after(theirs, got[0]), out_weight, FIRST)
    firsts = sum_over_z(part).reshape(count // NZ, 2 * FIRST)
    both = jnp.concatenate([slab[:, slice(*GROUPS[1])], opposite[:, slice(*GROUPS[1])]], axis=0)
    got.append(lax.ppermute(after(both, got[0]), "head", X_SWAP))
    sides, before = [], ()
    for i in range(len(GROUPS)):
        piece, across = got[i][:eighth], got[i][eighth:]
        piece = after(piece, theirs, *before)
        near, far = (lax.ppermute(piece, "dp", y_shift(k)) for k in (1, -1))
        if i == 0:
            across = lax.ppermute(piece, "dp", y_shift(2))
        before = (near, far, across)
        own = after(jnp.concatenate([piece, far, across, near], axis=0), came)
        sides.append((own, lax.ppermute(own, "dp", CORE_SWAP)))
    part = project(kept, after(given, got[1], *before), out_weight, 0, *sides[0], ())
    part = project(kept, given, out_weight, 1, *sides[1], (part,))
    rest = sum_over_z(part)
    swapped = lax.ppermute(firsts[:, FIRST:], "head", X_SWAP)
    begin = (firsts[:, :FIRST].astype(F32) + swapped.astype(F32)).astype(BF)
    attended = jnp.zeros((count // NZ, out_weight.shape[1]), BF)
    for lo, piece in ((0, begin), (FIRST, rest)):
        attended = lax.dynamic_update_slice(attended, piece, (0, lo))
    victim_blocks, targets, free_order, _ = lax.optimization_barrier(
        (victim_blocks, destinations[:, 0], free_slots[0], part)
    )
    new_pool = migrate(key_rows, value_rows, cache_pool, victim_blocks, targets, free_order)
    return (attended, new_pool)


def solution(mesh):
    return jax.shard_map(
        on_device,
        mesh=mesh,
        in_specs=(
            P("dp", "head"),
            P("dp", None),
            P("dp", None),
            P("head", None),
            P("dp", None),
            P("dp", None, None, "head"),
            P("dp"),
            P("dp", None),
            P("dp", None),
        ),
        out_specs=(P(("dp", "head"), None), P("dp", None, None, "head")),
        check_vma=False,
    )
```

```python
import functools
import math

import jax
import jax.numpy as jnp
from jax import lax
from jax.experimental import pallas as pl
from jax.experimental.pallas import tpu as pltpu
from jax.sharding import PartitionSpec as P

HD = 128
KVH = 8
BT = 16
NZ = 8
NY = 4
QB = 256
SPAN = 768
FIRST = 2048
GROUPS = ((2048, 5120), (5120, 8192))
Z_GROUPS = [[a * 8 + z for z in range(8)] for a in range(2)]
TILE = 1024
VMEM = 56 * 1024 * 1024
BF = jnp.bfloat16
F32 = jnp.float32
X_SWAP = [(i, (i + 8) % 16) for i in range(16)]
CORE_SWAP = [(i, i ^ 1) for i in range(16)]
LO_SWAP = [(i, i ^ 2) for i in range(16)]

def y_shift(k):
    return [(y * 4 + r, (y + k) % NY * 4 + r) for y in range(NY) for r in range(4)]


def attend_kernel(side, info, lengths, q_ref, k_ref, v_ref, o_ref):
    block = info[side] * 2 + pl.program_id(0)

    def attend(span):
        base = jnp.maximum(block - 2, 0) * QB
        rows = block * QB + lax.broadcasted_iota(jnp.int32, (QB, 1), 0)
        start = jnp.zeros((QB, 1), jnp.int32)
        end = 0
        for s in range(lengths.shape[1]):
            end = end + lengths[0, s]
            start = jnp.where(rows >= end, end, start)
        cols = base + lax.broadcasted_iota(jnp.int32, (QB, span), 1)
        bias = jnp.where((cols >= start) & (cols <= rows), 0.0, -1e30)
        keys = k_ref[pl.ds(pl.multiple_of(base, QB), span), :]
        values = jnp.concatenate(
            [v_ref[pl.ds(pl.multiple_of(base, QB), span), :], jnp.ones((span, HD), BF)], axis=1
        )
        for h in range(q_ref.shape[1] // HD):
            q = q_ref[:, h * HD : (h + 1) * HD]
            s = lax.dot_general(q, keys, (((1,), (1,)), ((), ())), preferred_element_type=F32) + bias
            top = jnp.max(s, axis=1, keepdims=True)
            e = jnp.exp2((s - top) * (math.log2(math.e) / math.sqrt(HD)))
            o = jnp.dot(e.astype(BF), values, preferred_element_type=F32)
            o_ref[:, h * HD : (h + 1) * HD] = (o[:, :HD] / o[:, HD:]).astype(BF)

    pl.when(block == 0)(lambda: attend(QB))
    pl.when(block == 1)(lambda: attend(2 * QB))
    pl.when(block >= 2)(lambda: attend(SPAN))


def attend_half(side, info, prompt_lengths, query_rows, key_rows, value_rows):
    count, width = query_rows.shape
    return pl.pallas_call(
        functools.partial(attend_kernel, side),
        grid_spec=pltpu.PrefetchScalarGridSpec(
            num_scalar_prefetch=2,
            grid=(2,),
            in_specs=[
                pl.BlockSpec((QB, width), lambda i, info, _: (info[side] * 2 + i, 0)),
                pl.BlockSpec((count, HD), lambda i, info, _: (0, info[2])),
                pl.BlockSpec((count, HD), lambda i, info, _: (0, info[2])),
            ],
            out_specs=pl.BlockSpec((QB, width), lambda i, info, _: (i, 0)),
        ),
        out_shape=jax.ShapeDtypeStruct((2 * QB, width), BF),
        compiler_params=pltpu.CompilerParams(vmem_limit_bytes=VMEM),
        cost_estimate=pl.CostEstimate(
            flops=4 * 2 * QB * SPAN * width, bytes_accessed=2 << 20, transcendentals=8 * QB * SPAN
        ),
    )(info, prompt_lengths, query_rows, key_rows, value_rows)


def after(value, *earlier):
    return lax.optimization_barrier((value, *earlier))[0]


def project_kernel(kept_ref, given_ref, w_ref, own_ref, other_ref, *refs):
    o_ref = refs[-1]
    half = own_ref.shape[0]
    acc = jnp.dot(kept_ref[...], w_ref[...], preferred_element_type=F32)
    acc += jnp.dot(given_ref[:, :half], own_ref[...], preferred_element_type=F32)
    acc += jnp.dot(given_ref[:, half:], other_ref[...], preferred_element_type=F32)
    o_ref[...] = acc.astype(BF)


def project(kept, given, out_weight, group, own, other, filled):
    rows, depth = kept.shape
    first, last = GROUPS[group]
    base = GROUPS[0][0]
    return pl.pallas_call(
        project_kernel,
        grid=((last - first) // TILE,),
        in_specs=[
            pl.BlockSpec((rows, depth), lambda i: (0, 0)),
            pl.BlockSpec((rows, depth), lambda i: (0, 0)),
            pl.BlockSpec((depth, TILE), lambda i: (0, first // TILE + i)),
            pl.BlockSpec((depth // 2, TILE), lambda i: (0, i)),
            pl.BlockSpec((depth // 2, TILE), lambda i: (0, i)),
        ]
        + [pl.BlockSpec(memory_space=pl.ANY)] * len(filled),
        out_specs=pl.BlockSpec((rows, TILE), lambda i: (0, (first - base) // TILE + i)),
        out_shape=jax.ShapeDtypeStruct((rows, GROUPS[-1][1] - base), BF),
        input_output_aliases={5: 0} if filled else {},
        compiler_params=pltpu.CompilerParams(vmem_limit_bytes=VMEM),
        cost_estimate=pl.CostEstimate(
            flops=4 * rows * depth * (last - first), bytes_accessed=6 * depth * (last - first), transcendentals=0
        ),
    )(kept, given, out_weight, own, other, *filled)


def project_first_kernel(kept_ref, theirs_ref, w_ref, o_ref):
    own = pl.program_id(0) == 0
    rows = jnp.where(own, kept_ref[...], theirs_ref[...])
    o_ref[...] = jnp.dot(rows, w_ref[...], preferred_element_type=F32).astype(BF)


def project_first(kept, theirs, out_weight, size):
    rows, depth = kept.shape
    tiles = size // TILE
    return pl.pallas_call(
        project_first_kernel,
        grid=(2, tiles),
        in_specs=[
            pl.BlockSpec((rows, depth), lambda h, i: (0, 0)),
            pl.BlockSpec((rows, depth), lambda h, i: (0, 0)),
            pl.BlockSpec((depth, TILE), lambda h, i: (0, i)),
        ],
        out_specs=pl.BlockSpec((rows, TILE), lambda h, i: (0, h * tiles + i)),
        out_shape=jax.ShapeDtypeStruct((rows, 2 * size), BF),
        compiler_params=pltpu.CompilerParams(vmem_limit_bytes=VMEM),
        cost_estimate=pl.CostEstimate(
            flops=4 * rows * depth * size, bytes_accessed=3 * depth * size * 2, transcendentals=0
        ),
    )(kept, theirs, out_weight)


def put_columns(array, piece, at):
    rows, size = piece.shape
    parts = [pl.ds(first, TILE) for first in range(0, size, TILE)]

    def kernel(_, piece_ref, o_ref, held, came, gone):
        reads = [pltpu.make_async_copy(piece_ref.at[:, p], held.at[:, p], came.at[i]) for i, p in enumerate(parts)]
        writes = [
            pltpu.make_async_copy(held.at[:, p], o_ref.at[:, pl.ds(at + i * TILE, TILE)], gone.at[i])
            for i, p in enumerate(parts)
        ]
        for read in reads:
            read.start()
        for read, write in zip(reads, writes):
            read.wait()
            write.start()
        for write in writes:
            write.wait()

    return pl.pallas_call(
        kernel,
        in_specs=[pl.BlockSpec(memory_space=pl.ANY)] * 2,
        out_specs=pl.BlockSpec(memory_space=pl.ANY),
        out_shape=jax.ShapeDtypeStruct(array.shape, array.dtype),
        scratch_shapes=[
            pltpu.VMEM((rows, size), BF),
            pltpu.SemaphoreType.DMA((len(parts),)),
            pltpu.SemaphoreType.DMA((len(parts),)),
        ],
        input_output_aliases={0: 0},
        compiler_params=pltpu.CompilerParams(vmem_limit_bytes=VMEM),
    )(array, piece)


def sum_over_z(part):
    return lax.psum_scatter(part, "head", scatter_dimension=0, axis_index_groups=Z_GROUPS, tiled=True)


def migrate(key_rows, value_rows, cache_pool, victim_blocks, targets, free_order):
    count, width = key_rows.shape[0], cache_pool.shape[3]
    pool, written = cache_pool.shape[0], count // BT
    at = lax.axis_index("head") * width
    me = lax.axis_index("dp")
    y, low = me // 4, me % 4
    at, half = after(jnp.stack([at, jnp.int32(written)]), targets)
    rows = [lax.dynamic_slice_in_dim(a, at, width, 1) for a in (key_rows, value_rows)]
    unwritten = lax.dynamic_slice_in_dim(cache_pool, half, pool - written, 0)
    span = jnp.stack([a.reshape(written, BT, width) for a in rows], axis=1)
    r = jnp.arange(16, dtype=jnp.int32)
    target_place = ((targets // 4 - y) % NY) * 4 + ((targets % 4) ^ low)
    same = targets[:, None] == targets[None, :]
    victims = victim_blocks.shape[0]
    order = jnp.arange(victims, dtype=jnp.int32)
    local_rank = jnp.sum((same & (order[None, :] < order[:, None])).astype(jnp.int32), axis=1)
    slot_of = target_place * 8 + local_rank
    lanes = jnp.arange(128, dtype=jnp.int32)
    picks = (slot_of[None, :] == lanes[:, None]).astype(BF)
    blocks = (victim_blocks[:, None] == jnp.arange(pool, dtype=jnp.int32)[None, :]).astype(BF)
    pick = jnp.dot(picks, blocks, preferred_element_type=F32).astype(BF)
    empty = 1.0 - jnp.sum(pick.astype(F32), axis=1)
    sending = jnp.einsum("sb,bktf->sktf", pick[:, :written], span, preferred_element_type=F32)
    sending = sending + jnp.einsum("sb,bktf->sktf", pick[:, written:], unwritten, preferred_element_type=F32)
    sending = (sending + 256.0 * empty[:, None, None, None]).astype(BF)
    b = sending.reshape(NY, 2, 2, 8 * 2 * BT * width)
    b = jnp.stack([b[:, :, 0], lax.ppermute(b[:, :, 1], "dp", CORE_SWAP)], axis=2)
    b = jnp.stack([b[:, 0], lax.ppermute(b[:, 1], "dp", LO_SWAP)], axis=1)
    b = jnp.stack([b[0]] + [lax.ppermute(b[k], "dp", y_shift(k)) for k in (1, 2, 3)])
    arrived = b.reshape(128, 2, BT, width)
    valid = (arrived[:, 0, 0, 0].astype(F32) < 100.0).reshape(16, 8)
    source = ((y - r // 4) % NY) * 4 + ((r % 4) ^ low)
    counts = jnp.sum(valid.astype(jnp.int32), axis=1)
    before = jnp.sum(jnp.where(source[None, :] < source[:, None], counts[None, :], 0), axis=1)
    ranks = before[:, None] + jnp.arange(8, dtype=jnp.int32)[None, :]
    rank_of_slot = jnp.sum(
        (free_order[None, :] == jnp.arange(pool, dtype=jnp.int32)[:, None]) * jnp.arange(pool, dtype=jnp.int32)[None, :],
        axis=1,
    )
    hits = (ranks.reshape(128, 1) == rank_of_slot[None, :]) & valid.reshape(128, 1)
    taken = jnp.sum(hits.astype(jnp.int32), axis=0) > 0
    fresh = jnp.einsum(
        "sktf,sb->bktf", jnp.where(valid.reshape(128, 1, 1, 1), arrived, 0), hits.astype(BF), preferred_element_type=F32
    ).astype(BF)
    sectioned = jnp.concatenate([span, unwritten], axis=0)
    return jnp.where(taken[:, None, None, None], fresh, sectioned)


def on_device(
    query_rows,
    key_rows,
    value_rows,
    out_weight,
    prompt_lengths,
    cache_pool,
    victim_blocks,
    destinations,
    free_slots,
):
    head, me = lax.axis_index("head"), lax.axis_index("dp")
    z, hi = head % NZ, head // NZ
    y, core = me // 4, me % 2
    depth = out_weight.shape[0]
    eighth = depth // 8
    slab = lax.dynamic_slice_in_dim(out_weight, (y * 2 + core) * eighth, eighth, 0)
    kv = head * KVH // lax.axis_size("head")
    place = jnp.arange(depth, dtype=jnp.int32)
    slot = place // eighth
    taken_from = (((y + slot % NY) % NY) * 2 + (core ^ (slot // NY))) * eighth + place % eighth
    order = (place[:, None] == taken_from[None, :]).astype(BF)
    info = jnp.stack([1 - hi, hi, kv])
    count = query_rows.shape[0] // 2
    got = [lax.ppermute(slab[:, slice(*GROUPS[0])], "head", X_SWAP)]
    opposite = lax.dynamic_slice_in_dim(after(out_weight, got[0]), ((y + 2) % NY * 2 + core) * eighth, eighth, 0)
    theirs = attend_half(0, info, prompt_lengths, query_rows, key_rows, value_rows)
    came = lax.ppermute(theirs, "head", X_SWAP)
    kept = attend_half(1, info, after(prompt_lengths, theirs), query_rows, key_rows, value_rows)
    given = jnp.dot(came, order, preferred_element_type=F32).astype(BF)
    part = project_first(kept, after(theirs, got[0]), out_weight, FIRST)
    firsts = sum_over_z(part).reshape(count // NZ, 2 * FIRST)
    both = jnp.concatenate([slab[:, slice(*GROUPS[1])], opposite[:, slice(*GROUPS[1])]], axis=0)
    got.append(lax.ppermute(after(both, got[0]), "head", X_SWAP))
    sides, before = [], ()
    for i in range(len(GROUPS)):
        piece, across = got[i][:eighth], got[i][eighth:]
        piece = after(piece, theirs, *before)
        near, far = (lax.ppermute(piece, "dp", y_shift(k)) for k in (1, -1))
        if i == 0:
            across = lax.ppermute(piece, "dp", y_shift(2))
        before = (near, far, across)
        own = after(jnp.concatenate([piece, far, across, near], axis=0), came)
        sides.append((own, lax.ppermute(own, "dp", CORE_SWAP)))
    part = project(kept, after(given, got[1], *before), out_weight, 0, *sides[0], ())
    part = project(kept, given, out_weight, 1, *sides[1], (part,))
    rest = sum_over_z(part)
    swapped = lax.ppermute(firsts[:, FIRST:], "head", X_SWAP)
    begin = (firsts[:, :FIRST].astype(F32) + swapped.astype(F32)).astype(BF)
    begin = jnp.pad(begin, ((0, 0), (0, out_weight.shape[1] - FIRST)))
    attended = put_columns(begin, rest, FIRST)
    victim_blocks, targets, free_order, _ = lax.optimization_barrier(
        (victim_blocks, destinations[:, 0], free_slots[0], part)
    )
    new_pool = migrate(key_rows, value_rows, cache_pool, victim_blocks, targets, free_order)
    return (attended, new_pool)


def solution(mesh):
    return jax.shard_map(
        on_device,
        mesh=mesh,
        in_specs=(
            P("dp", "head"),
            P("dp", None),
            P("dp", None),
            P("head", None),
            P("dp", None),
            P("dp", None, None, "head"),
            P("dp"),
            P("dp", None),
            P("dp", None),
        ),
        out_specs=(P(("dp", "head"), None), P("dp", None, None, "head")),
        check_vma=False,
    )
```

```python
import functools
import math

import jax
import jax.numpy as jnp
from jax import lax
from jax.experimental import pallas as pl
from jax.experimental.pallas import tpu as pltpu
from jax.sharding import PartitionSpec as P

HD = 128
KVH = 8
BT = 16
NZ = 8
NY = 4
QB = 256
SPAN = 768
FIRST = 2048
GROUPS = ((2048, 5120), (5120, 8192))
Z_GROUPS = [[a * 8 + z for z in range(8)] for a in range(2)]
TILE = 1024
VMEM = 56 * 1024 * 1024
BF = jnp.bfloat16
F32 = jnp.float32
X_SWAP = [(i, (i + 8) % 16) for i in range(16)]
CORE_SWAP = [(i, i ^ 1) for i in range(16)]
LO_SWAP = [(i, i ^ 2) for i in range(16)]

def y_shift(k):
    return [(y * 4 + r, (y + k) % NY * 4 + r) for y in range(NY) for r in range(4)]


def attend_kernel(side, info, lengths, q_ref, k_ref, v_ref, o_ref):
    block = info[side] * 2 + pl.program_id(0)

    def attend(span):
        base = jnp.maximum(block - 2, 0) * QB
        rows = block * QB + lax.broadcasted_iota(jnp.int32, (QB, 1), 0)
        start = jnp.zeros((QB, 1), jnp.int32)
        end = 0
        for s in range(lengths.shape[1]):
            end = end + lengths[0, s]
            start = jnp.where(rows >= end, end, start)
        cols = base + lax.broadcasted_iota(jnp.int32, (QB, span), 1)
        bias = jnp.where((cols >= start) & (cols <= rows), 0.0, -1e30)
        keys = k_ref[pl.ds(pl.multiple_of(base, QB), span), :]
        values = jnp.concatenate(
            [v_ref[pl.ds(pl.multiple_of(base, QB), span), :], jnp.ones((span, HD), BF)], axis=1
        )
        for h in range(q_ref.shape[1] // HD):
            q = q_ref[:, h * HD : (h + 1) * HD]
            s = lax.dot_general(q, keys, (((1,), (1,)), ((), ())), preferred_element_type=F32) + bias
            top = jnp.max(s, axis=1, keepdims=True)
            e = jnp.exp2((s - top) * (math.log2(math.e) / math.sqrt(HD)))
            o = jnp.dot(e.astype(BF), values, preferred_element_type=F32)
            o_ref[:, h * HD : (h + 1) * HD] = (o[:, :HD] / o[:, HD:]).astype(BF)

    pl.when(block == 0)(lambda: attend(QB))
    pl.when(block == 1)(lambda: attend(2 * QB))
    pl.when(block >= 2)(lambda: attend(SPAN))


def attend_half(side, info, prompt_lengths, query_rows, key_rows, value_rows):
    count, width = query_rows.shape
    return pl.pallas_call(
        functools.partial(attend_kernel, side),
        grid_spec=pltpu.PrefetchScalarGridSpec(
            num_scalar_prefetch=2,
            grid=(2,),
            in_specs=[
                pl.BlockSpec((QB, width), lambda i, info, _: (info[side] * 2 + i, 0)),
                pl.BlockSpec((count, HD), lambda i, info, _: (0, info[2])),
                pl.BlockSpec((count, HD), lambda i, info, _: (0, info[2])),
            ],
            out_specs=pl.BlockSpec((QB, width), lambda i, info, _: (i, 0)),
        ),
        out_shape=jax.ShapeDtypeStruct((2 * QB, width), BF),
        compiler_params=pltpu.CompilerParams(vmem_limit_bytes=VMEM),
        cost_estimate=pl.CostEstimate(
            flops=4 * 2 * QB * SPAN * width, bytes_accessed=2 << 20, transcendentals=8 * QB * SPAN
        ),
    )(info, prompt_lengths, query_rows, key_rows, value_rows)


def after(value, *earlier):
    return lax.optimization_barrier((value, *earlier))[0]


def project_kernel(kept_ref, given_ref, w_ref, own_ref, other_ref, *refs):
    o_ref = refs[-1]
    half = own_ref.shape[0]
    acc = jnp.dot(kept_ref[...], w_ref[...], preferred_element_type=F32)
    acc += jnp.dot(given_ref[:, :half], own_ref[...], preferred_element_type=F32)
    acc += jnp.dot(given_ref[:, half:], other_ref[...], preferred_element_type=F32)
    o_ref[...] = acc.astype(BF)


def project(kept, given, out_weight, group, own, other, filled):
    rows, depth = kept.shape
    first, last = GROUPS[group]
    base = GROUPS[0][0]
    return pl.pallas_call(
        project_kernel,
        grid=((last - first) // TILE,),
        in_specs=[
            pl.BlockSpec((rows, depth), lambda i: (0, 0)),
            pl.BlockSpec((rows, depth), lambda i: (0, 0)),
            pl.BlockSpec((depth, TILE), lambda i: (0, first // TILE + i)),
            pl.BlockSpec((depth // 2, TILE), lambda i: (0, i)),
            pl.BlockSpec((depth // 2, TILE), lambda i: (0, i)),
        ]
        + [pl.BlockSpec(memory_space=pl.ANY)] * len(filled),
        out_specs=pl.BlockSpec((rows, TILE), lambda i: (0, (first - base) // TILE + i)),
        out_shape=jax.ShapeDtypeStruct((rows, GROUPS[-1][1] - base), BF),
        input_output_aliases={5: 0} if filled else {},
        compiler_params=pltpu.CompilerParams(vmem_limit_bytes=VMEM),
        cost_estimate=pl.CostEstimate(
            flops=4 * rows * depth * (last - first), bytes_accessed=6 * depth * (last - first), transcendentals=0
        ),
    )(kept, given, out_weight, own, other, *filled)


def project_first_kernel(kept_ref, theirs_ref, w_ref, o_ref):
    own = pl.program_id(0) == 0
    rows = jnp.where(own, kept_ref[...], theirs_ref[...])
    o_ref[...] = jnp.dot(rows, w_ref[...], preferred_element_type=F32).astype(BF)


def project_first(kept, theirs, out_weight, size):
    rows, depth = kept.shape
    tiles = size // TILE
    return pl.pallas_call(
        project_first_kernel,
        grid=(2, tiles),
        in_specs=[
            pl.BlockSpec((rows, depth), lambda h, i: (0, 0)),
            pl.BlockSpec((rows, depth), lambda h, i: (0, 0)),
            pl.BlockSpec((depth, TILE), lambda h, i: (0, i)),
        ],
        out_specs=pl.BlockSpec((rows, TILE), lambda h, i: (0, h * tiles + i)),
        out_shape=jax.ShapeDtypeStruct((rows, 2 * size), BF),
        compiler_params=pltpu.CompilerParams(vmem_limit_bytes=VMEM),
        cost_estimate=pl.CostEstimate(
            flops=4 * rows * depth * size, bytes_accessed=3 * depth * size * 2, transcendentals=0
        ),
    )(kept, theirs, out_weight)


def put_columns(array, piece, at):
    rows, size = piece.shape
    width = 2 * TILE
    parts = [pl.ds(first, width) for first in range(0, size, width)]

    def kernel(_, piece_ref, o_ref, held, came, gone):
        reads = [pltpu.make_async_copy(piece_ref.at[:, p], held.at[:, p], came.at[i]) for i, p in enumerate(parts)]
        writes = [
            pltpu.make_async_copy(held.at[:, p], o_ref.at[:, pl.ds(at + i * width, width)], gone.at[i])
            for i, p in enumerate(parts)
        ]
        for read in reads:
            read.start()
        for read, write in zip(reads, writes):
            read.wait()
            write.start()
        for write in writes:
            write.wait()

    return pl.pallas_call(
        kernel,
        in_specs=[pl.BlockSpec(memory_space=pl.ANY)] * 2,
        out_specs=pl.BlockSpec(memory_space=pl.ANY),
        out_shape=jax.ShapeDtypeStruct(array.shape, array.dtype),
        scratch_shapes=[
            pltpu.VMEM((rows, size), BF),
            pltpu.SemaphoreType.DMA((len(parts),)),
            pltpu.SemaphoreType.DMA((len(parts),)),
        ],
        input_output_aliases={0: 0},
        compiler_params=pltpu.CompilerParams(vmem_limit_bytes=VMEM),
    )(array, piece)


def sum_over_z(part):
    return lax.psum_scatter(part, "head", scatter_dimension=0, axis_index_groups=Z_GROUPS, tiled=True)


def migrate(key_rows, value_rows, cache_pool, victim_blocks, targets, free_order):
    count, width = key_rows.shape[0], cache_pool.shape[3]
    pool, written = cache_pool.shape[0], count // BT
    at = lax.axis_index("head") * width
    me = lax.axis_index("dp")
    y, low = me // 4, me % 4
    at, half = after(jnp.stack([at, jnp.int32(written)]), targets)
    rows = [lax.dynamic_slice_in_dim(a, at, width, 1) for a in (key_rows, value_rows)]
    unwritten = lax.dynamic_slice_in_dim(cache_pool, half, pool - written, 0)
    span = jnp.stack([a.reshape(written, BT, width) for a in rows], axis=1)
    r = jnp.arange(16, dtype=jnp.int32)
    target_place = ((targets // 4 - y) % NY) * 4 + ((targets % 4) ^ low)
    same = targets[:, None] == targets[None, :]
    victims = victim_blocks.shape[0]
    order = jnp.arange(victims, dtype=jnp.int32)
    local_rank = jnp.sum((same & (order[None, :] < order[:, None])).astype(jnp.int32), axis=1)
    slot_of = target_place * 8 + local_rank
    lanes = jnp.arange(128, dtype=jnp.int32)
    picks = (slot_of[None, :] == lanes[:, None]).astype(BF)
    blocks = (victim_blocks[:, None] == jnp.arange(pool, dtype=jnp.int32)[None, :]).astype(BF)
    pick = jnp.dot(picks, blocks, preferred_element_type=F32).astype(BF)
    empty = 1.0 - jnp.sum(pick.astype(F32), axis=1)
    sending = jnp.einsum("sb,bktf->sktf", pick[:, :written], span, preferred_element_type=F32)
    sending = sending + jnp.einsum("sb,bktf->sktf", pick[:, written:], unwritten, preferred_element_type=F32)
    sending = (sending + 256.0 * empty[:, None, None, None]).astype(BF)
    b = sending.reshape(NY, 2, 2, 8 * 2 * BT * width)
    b = jnp.stack([b[:, :, 0], lax.ppermute(b[:, :, 1], "dp", CORE_SWAP)], axis=2)
    b = jnp.stack([b[:, 0], lax.ppermute(b[:, 1], "dp", LO_SWAP)], axis=1)
    b = jnp.stack([b[0]] + [lax.ppermute(b[k], "dp", y_shift(k)) for k in (1, 2, 3)])
    arrived = b.reshape(128, 2, BT, width)
    valid = (arrived[:, 0, 0, 0].astype(F32) < 100.0).reshape(16, 8)
    source = ((y - r // 4) % NY) * 4 + ((r % 4) ^ low)
    counts = jnp.sum(valid.astype(jnp.int32), axis=1)
    before = jnp.sum(jnp.where(source[None, :] < source[:, None], counts[None, :], 0), axis=1)
    ranks = before[:, None] + jnp.arange(8, dtype=jnp.int32)[None, :]
    rank_of_slot = jnp.sum(
        (free_order[None, :] == jnp.arange(pool, dtype=jnp.int32)[:, None]) * jnp.arange(pool, dtype=jnp.int32)[None, :],
        axis=1,
    )
    hits = (ranks.reshape(128, 1) == rank_of_slot[None, :]) & valid.reshape(128, 1)
    taken = jnp.sum(hits.astype(jnp.int32), axis=0) > 0
    fresh = jnp.einsum(
        "sktf,sb->bktf", jnp.where(valid.reshape(128, 1, 1, 1), arrived, 0), hits.astype(BF), preferred_element_type=F32
    ).astype(BF)
    sectioned = jnp.concatenate([span, unwritten], axis=0)
    return jnp.where(taken[:, None, None, None], fresh, sectioned)


def on_device(
    query_rows,
    key_rows,
    value_rows,
    out_weight,
    prompt_lengths,
    cache_pool,
    victim_blocks,
    destinations,
    free_slots,
):
    head, me = lax.axis_index("head"), lax.axis_index("dp")
    z, hi = head % NZ, head // NZ
    y, core = me // 4, me % 2
    depth = out_weight.shape[0]
    eighth = depth // 8
    slab = lax.dynamic_slice_in_dim(out_weight, (y * 2 + core) * eighth, eighth, 0)
    kv = head * KVH // lax.axis_size("head")
    place = jnp.arange(depth, dtype=jnp.int32)
    slot = place // eighth
    taken_from = (((y + slot % NY) % NY) * 2 + (core ^ (slot // NY))) * eighth + place % eighth
    order = (place[:, None] == taken_from[None, :]).astype(BF)
    info = jnp.stack([1 - hi, hi, kv])
    count = query_rows.shape[0] // 2
    got = [lax.ppermute(slab[:, slice(*GROUPS[0])], "head", X_SWAP)]
    opposite = lax.dynamic_slice_in_dim(after(out_weight, got[0]), ((y + 2) % NY * 2 + core) * eighth, eighth, 0)
    theirs = attend_half(0, info, prompt_lengths, query_rows, key_rows, value_rows)
    came = lax.ppermute(theirs, "head", X_SWAP)
    kept = attend_half(1, info, after(prompt_lengths, theirs), query_rows, key_rows, value_rows)
    given = jnp.dot(came, order, preferred_element_type=F32).astype(BF)
    part = project_first(kept, after(theirs, got[0]), out_weight, FIRST)
    firsts = sum_over_z(part).reshape(count // NZ, 2 * FIRST)
    both = jnp.concatenate([slab[:, slice(*GROUPS[1])], opposite[:, slice(*GROUPS[1])]], axis=0)
    got.append(lax.ppermute(after(both, got[0]), "head", X_SWAP))
    sides, before = [], ()
    for i in range(len(GROUPS)):
        piece, across = got[i][:eighth], got[i][eighth:]
        piece = after(piece, theirs, *before)
        near, far = (lax.ppermute(piece, "dp", y_shift(k)) for k in (1, -1))
        if i == 0:
            across = lax.ppermute(piece, "dp", y_shift(2))
        before = (near, far, across)
        own = after(jnp.concatenate([piece, far, across, near], axis=0), came)
        sides.append((own, lax.ppermute(own, "dp", CORE_SWAP)))
    part = project(kept, after(given, got[1], *before), out_weight, 0, *sides[0], ())
    part = project(kept, given, out_weight, 1, *sides[1], (part,))
    rest = sum_over_z(part)
    swapped = lax.ppermute(firsts[:, FIRST:], "head", X_SWAP)
    begin = (firsts[:, :FIRST].astype(F32) + swapped.astype(F32)).astype(BF)
    begin = jnp.pad(begin, ((0, 0), (0, out_weight.shape[1] - FIRST)))
    attended = put_columns(begin, rest, FIRST)
    victim_blocks, targets, free_order, _ = lax.optimization_barrier(
        (victim_blocks, destinations[:, 0], free_slots[0], part)
    )
    new_pool = migrate(key_rows, value_rows, cache_pool, victim_blocks, targets, free_order)
    return (attended, new_pool)


def solution(mesh):
    return jax.shard_map(
        on_device,
        mesh=mesh,
        in_specs=(
            P("dp", "head"),
            P("dp", None),
            P("dp", None),
            P("head", None),
            P("dp", None),
            P("dp", None, None, "head"),
            P("dp"),
            P("dp", None),
            P("dp", None),
        ),
        out_specs=(P(("dp", "head"), None), P("dp", None, None, "head")),
        check_vma=False,
    )
```
